512 devices in a mesh: line: 256 (over x, y, z), rhs: 2 (over core).
Axes of the slice: x: 4, y: 8, z: 8, core: 2. Of those that a mesh axis runs over, the one named last changes fastest.
Arguments:
- diag_blocks: float32 [256, 256, 256], P('line'), may hold values from -1 to 6, as said below
- lower_blocks: float32 [256, 256, 256], P('line'), may hold values from -1.7 to 1.7
- right_sides: float32 [256, 256, 64], P('line', None, 'rhs'), may hold values from -1.5 to 1.5
Outputs:
- solution: float32 [256, 256, 64], P('line', None, 'rhs')
The draws below stay inside these ranges and needn't reach their ends.
Inputs may be any that keep to these rules, and one draw needn't show every extreme that they name: `diag_blocks`: each diagonal block is symmetric, and K is symmetric positive definite.
All inputs are finite; a program needn't handle non-finite values.
Results may differ from the reference program's by a relative error of at most 0.0013.
Values sent between devices are 32-bit elements; how exact they have to be, the bound alone decides.
No kernel may reach another device: no remote copies, remote signals or barrier semaphores. Data moves between devices by JAX's collectives and lax.ppermute only.
A program may use at most 64 MiB of HBM per device.

```python
import math
import jax
import jax.numpy as jnp
from jax import lax

ORDER = 256
BLOCKS = 256
RHS = 64


def edge_weights(key, low_end, high_end):
    low_side = jax.random.uniform(jax.random.fold_in(key, 101), (BLOCKS, ORDER), jnp.float32, low_end, high_end)
    high_side = jax.random.uniform(jax.random.fold_in(key, 102), (BLOCKS, ORDER), jnp.float32, low_end, high_end)
    return (low_side, high_side)


def rotation_blocks(key):
    angles = jax.random.uniform(jax.random.fold_in(key, 7), (BLOCKS, ORDER // 2), jnp.float32, -math.pi, math.pi)
    shuffle = jax.vmap(lambda sub_key: jax.random.permutation(sub_key, ORDER))(jax.random.split(jax.random.fold_in(key, 8), BLOCKS))
    row_index = jnp.arange(ORDER)[:, None]
    col_index = jnp.arange(ORDER)[None, :]
    cos_row = jnp.repeat(jnp.cos(angles), 2, axis=1)[:, :, None]
    sin_row = jnp.repeat(jnp.sin(angles), 2, axis=1)[:, :, None]
    pair_sign = jnp.where(row_index % 2 == 0, -1.0, 1.0)
    same_pair = row_index // 2 == col_index // 2
    on_diagonal = row_index == col_index
    rotation = jnp.where(on_diagonal, cos_row, jnp.where(same_pair, pair_sign * sin_row, 0.0))
    return jax.vmap(lambda block, picks: block[picks])(rotation, shuffle)


def draw_lower_blocks(key, part):
    low_side, high_side = edge_weights(key, 0.5, 1.5)
    key = jax.random.fold_in(key, 1)
    ortho = rotation_blocks(key)
    return -(jnp.sqrt(high_side)[:, :, None] * ortho * jnp.sqrt(low_side)[:, None, :])


def draw_diag_blocks(key, part):
    low_side, high_side = edge_weights(key, 0.5, 1.5)
    margin_low, margin_high = (2.0, 40.0)
    mixing_low, mixing_high = (2.0, 8.0)
    key = jax.random.fold_in(key, 2)
    unit = 1.0 / float(BLOCKS * BLOCKS)
    margin = unit * jnp.exp(jax.random.uniform(jax.random.fold_in(key, 3), (BLOCKS, ORDER), jnp.float32, math.log(margin_low), math.log(margin_high)))
    mixing = unit * jax.random.uniform(jax.random.fold_in(key, 4), (BLOCKS, 1, 1), jnp.float32, mixing_low, mixing_high)
    ortho = rotation_blocks(jax.random.fold_in(key, 5))
    diagonal = high_side + jnp.roll(low_side, -1, axis=0) + margin + 2.0 * mixing[:, :, 0]
    identity = jnp.eye(ORDER, dtype=jnp.float32)
    return diagonal[:, :, None] * identity - mixing * (ortho + jnp.swapaxes(ortho, 1, 2))


def draw_right_sides(key, part):
    key = jax.random.fold_in(key, 11)
    level = 8.0 * float(BLOCKS) ** (-1.5)
    values = jnp.clip(jax.random.normal(key, (BLOCKS, ORDER, RHS), jnp.float32), -4.0, 4.0)
    return values * level


def setup_inputs(seed: int = 0) -> dict:
    seeds = jax.random.split(jax.random.key(seed), 4)
    diag_blocks = draw_diag_blocks(jax.random.fold_in(seeds[3], 71), 0)
    lower_blocks = draw_lower_blocks(jax.random.fold_in(seeds[3], 71), 0)
    right_sides = draw_right_sides(jax.random.fold_in(seeds[3], 71), 0)
    return {"diag_blocks": diag_blocks, "lower_blocks": lower_blocks, "right_sides": right_sides}


def reference(diag_blocks, lower_blocks, right_sides):
    highest = lax.Precision.HIGHEST
    dtype = diag_blocks.dtype
    first = (jnp.arange(BLOCKS) == 0)[:, None, None]
    couplings = jnp.where(first, jnp.zeros_like(lower_blocks), lower_blocks)
    columns = right_sides.shape[2]

    def forward(carry, inputs):
        prev_diag, prev_source = carry
        diag_block, coupling, source = inputs
        joined = jnp.concatenate([coupling.T, prev_source], axis=1)
        solved = jnp.linalg.solve(prev_diag, joined)
        new_diag = diag_block - jnp.dot(coupling, solved[:, :ORDER], precision=highest)
        new_source = source - jnp.dot(coupling, solved[:, ORDER:], precision=highest)
        return ((new_diag, new_source), (new_diag, new_source))
    start = (jnp.eye(ORDER, dtype=dtype), jnp.zeros((ORDER, columns), dtype))
    unused, (reduced, sources) = lax.scan(forward, start, (diag_blocks, couplings, right_sides))
    upper_side = jnp.concatenate([couplings[1:], jnp.zeros_like(couplings[:1])], axis=0)

    def backward(later, inputs):
        reduced_block, source, upper = inputs
        answer = jnp.linalg.solve(reduced_block, source - jnp.dot(upper.T, later, precision=highest))
        return (answer, answer)
    unused_last, solution = lax.scan(backward, jnp.zeros((ORDER, columns), dtype), (reduced, sources, upper_side), reverse=True)
    return solution
```

```python
import functools
import jax
import jax.numpy as jnp
from jax import lax
from jax.experimental import pallas as pl
from jax.experimental.pallas import tpu as pltpu
from jax.sharding import PartitionSpec as P

F32 = jnp.float32
BF16 = jnp.bfloat16
BOTH = ("line", "rhs")
DOUBLINGS = (0, 4, 4, 4, 4, 4, 3, 1, 0)
RESIDUAL_MAX = 1.0e-2
SLOW_STEPS = 80


def split(x, terms):
    parts = []
    for i in range(terms):
        part = x.astype(BF16)
        parts.append(part)
        if i + 1 < terms:
            x = x - part.astype(F32)
    return parts


def one(a, b):
    return jnp.dot(a, b, preferred_element_type=F32)


def product(a, b):
    terms = len(a)
    total = None
    for order in range(terms - 1, -1, -1):
        for i in range(order + 1):
            term = one(a[i], b[order - i])
            total = term if total is None else total + term
    return total


def unit(n):
    rows = lax.broadcasted_iota(jnp.int32, (n, n), 0)
    cols = lax.broadcasted_iota(jnp.int32, (n, n), 1)
    return (rows == cols).astype(F32)


def left_lanes(rows, half):
    return lax.broadcasted_iota(jnp.int32, (rows, 2 * half), 1) < half


def pack(x, tail, out):
    n = x.shape[0]
    h = n // 2
    corner = x[h:, h:]
    left = left_lanes(h, h // 2)
    out[:, :h] = x[:, :h]
    out[:h, h:] = jnp.where(left, corner, tail[:h])
    out[h:, h:] = jnp.where(left, pltpu.roll(corner, h // 2, 1), tail[h:])


def unpack(m):
    n = m.shape[0]
    h = n // 2
    tail = m[:, h:]
    left = left_lanes(h, h // 2)
    corner = jnp.where(left, tail[:h], pltpu.roll(tail[h:], h // 2, 1))
    low = m[h:, :h]
    top = jnp.concatenate([m[:h, :h], low.T], axis=1)
    bottom = jnp.concatenate([low, corner], axis=1)
    return jnp.concatenate([top, bottom], axis=0), tail


def invert(d, guess, doublings, x_ref):
    identity = unit(d.shape[0])
    d_parts = split(d, 3)
    error = identity - product(d_parts[:2], split(guess, 2))
    power = error.astype(BF16)
    series = identity + error
    for _ in range(doublings):
        power = one(power, power).astype(BF16)
        series = series + one(series.astype(BF16), power)
    x = one(guess.astype(BF16), series.astype(BF16))
    x = 0.5 * (x + x.T)
    residual = identity - product(d_parts[:2], split(x, 2))
    x = x + one(x.astype(BF16), residual.astype(BF16))
    residual = identity - product(d_parts, split(x, 3))
    x_ref[...] = x + one(x.astype(BF16), residual.astype(BF16))
    size = jnp.sum(residual * residual)

    @pl.when(jnp.logical_not(size < RESIDUAL_MAX * RESIDUAL_MAX))
    def _():
        x_ref[...] = guess

        def keep_on(state):
            step, worst = state
            return jnp.logical_and(step < SLOW_STEPS, worst > 1.0e-6)

        def improve(state):
            step, _ = state
            x = x_ref[...]
            rest = identity - product(d_parts, split(x, 3))
            x = x + product(split(x, 3), split(rest, 3))
            x_ref[...] = 0.5 * (x + x.T)
            return step + 1, jnp.sum(rest * rest)

        lax.while_loop(keep_on, improve, (0, jnp.float32(1.0)))


def first_guess(d):
    identity = unit(d.shape[0])
    diagonal = jnp.sum(d * identity, axis=1, keepdims=True)
    reach = jnp.max(jnp.sum(jnp.abs(d), axis=1, keepdims=True) / diagonal)
    return identity * (jnp.minimum(1.0, 1.9 / reach) / diagonal)


def start_kernel(doublings, d_ref, b_ref, m_ref, x_ref, b_out):
    d = d_ref[...]
    invert(d, first_guess(d), doublings, x_ref)
    b0, b1 = b_ref[0], b_ref[1]
    b = jnp.concatenate([jnp.zeros((b0.shape[0], 2 * b0.shape[1]), F32), b0, b1], axis=1)
    b_out[...] = b
    x = x_ref[...]
    pack(x, product(split(x, 3), split(b, 3)), m_ref)


def reduce_rows(d_ref, b_ref, t_ref):
    n = d_ref.shape[0]
    first, first_tail = unpack(t_ref[:n])
    second, second_tail = unpack(t_ref[n:])
    b = b_ref[...] - first_tail - second_tail
    b = jnp.where(left_lanes(b.shape[0], b.shape[1] // 2), 0.0, b)
    return d_ref[...] - first - second, b


def level_kernel(doublings, d_ref, b_ref, t_ref, guess_ref, m_ref, x_ref, d_out, b_out):
    d, b = reduce_rows(d_ref, b_ref, t_ref)
    d_out[...] = d
    b_out[...] = b
    invert(d, guess_ref[...], doublings, x_ref)
    x = x_ref[...]
    pack(x, product(split(x, 3), split(b, 3)), m_ref)


def end_kernel(doublings, info, d_ref, b_ref, t_ref, guess_ref, out_ref, x_ref):
    d, b = reduce_rows(d_ref, b_ref, t_ref)
    invert(d, guess_ref[...], doublings, x_ref)
    answer = product(split(x_ref[...], 3), split(b, 3))
    w = out_ref.shape[1]
    out_ref[...] = jnp.where(info[1] == 0, answer[:, 2 * w : 3 * w], answer[:, 3 * w :])


def transfer(c, info, m_ref, t_ref):
    n = c.shape[0]
    m = jnp.where(info[1] == 0, m_ref[n:], m_ref[:n])
    x, tail = unpack(m)
    c_parts = split(c, 3)
    z = product(c_parts, split(x, 3))
    z_parts = split(z, 3)
    t = product(z_parts, split(c.T, 3))
    pack(t, product(c_parts, split(tail, 3)), t_ref)
    return z_parts


def first_coupling_kernel(info, m_ref, low_ref, near_ref, far_ref, t_ref, c_out):
    below = info[1] == 0
    c = jnp.where(below, low_ref[...], near_ref[...].T)
    c = jnp.where(jnp.logical_and(below, info[0] == 0), 0.0, c)
    far = far_ref[...]
    far = jnp.where(below, far, far.T)
    far = jnp.where(jnp.logical_and(below, info[0] == 1), 0.0, far)
    z_parts = transfer(c, info, m_ref, t_ref)
    c_out[...] = -product(z_parts, split(far, 3))


def coupling_kernel(info, m_ref, c_ref, far_ref, t_ref, c_out):
    z_parts = transfer(c_ref[...], info, m_ref, t_ref)
    c_out[...] = -product(z_parts, split(far_ref[...], 3))


def last_coupling_kernel(info, m_ref, c_ref, t_ref):
    transfer(c_ref[...], info, m_ref, t_ref)


def call(kernel, name, operands, outs, scratch=(), scalars=False):
    specs = [pl.BlockSpec(memory_space=pltpu.VMEM)] * (len(operands) - int(scalars))
    if scalars:
        specs = [pl.BlockSpec(memory_space=pltpu.SMEM)] + specs
    shapes = [jax.ShapeDtypeStruct(shape, F32) for shape in outs]
    return pl.pallas_call(
        kernel,
        name=name,
        in_specs=specs,
        out_specs=[pl.BlockSpec(memory_space=pltpu.VMEM)] * len(outs),
        out_shape=shapes,
        scratch_shapes=[pltpu.VMEM(shape, F32) for shape in scratch],
        compiler_params=pltpu.CompilerParams(vmem_limit_bytes=40 * 2**20),
    )(*operands)


def pairs(line, stride):
    if 2 * stride < line:
        return [[2 * p, 2 * ((p - stride) % line) + 1] for p in range(line)]
    real = [[2 * p, 2 * (p - stride) + 1] for p in range(stride, line)]
    quarter = line // 4
    idle = [[2 * p, 2 * (p + (3 * quarter if p < quarter else quarter)) + 1] for p in range(stride)]
    return real + idle


def outward(line, stride, core0, core1):
    route = []
    for p in range(line):
        if core0 and p + core0 * stride < line:
            route.append((2 * p, 2 * (p + core0 * stride)))
        if p - core1 * stride >= 0:
            route.append((2 * p + 1, 2 * (p - core1 * stride) + 1))
    return route


def on_device(diag_blocks, lower_blocks, right_sides):
    d, low, b = diag_blocks[0], lower_blocks[0], right_sides[0]
    n, w = b.shape
    line = lax.axis_size("line")
    info = jnp.stack([lax.axis_index("line"), lax.axis_index("rhs")]).astype(jnp.int32)
    near = lax.ppermute(low, BOTH, outward(line, 1, 0, 1))
    far = lax.ppermute(low, BOTH, outward(line, 1, 1, 2))
    sides = lax.all_gather(b, "rhs")
    square, tall = (n, n), (n, 4 * w)
    level, stride = 0, 1
    message, x, b = call(
        functools.partial(start_kernel, DOUBLINGS[0]), "start", (d, sides), (square, square, tall)
    )
    while stride < line:
        both = lax.all_gather(message, BOTH, axis_index_groups=pairs(line, stride), tiled=True)
        if stride == 1:
            term, c = call(
                first_coupling_kernel, "couple0", (info, both, low, near, far), (square, square), scalars=True
            )
        elif 2 * stride < line:
            far = lax.ppermute(c, BOTH, outward(line, stride, 1, 1))
            term, c = call(
                coupling_kernel, f"couple{level}", (info, both, c, far), (square, square), scalars=True
            )
        else:
            (term,) = call(
                last_coupling_kernel, f"couple{level}", (info, both, c), (square,), scalars=True
            )
        terms = lax.all_gather(term, "rhs", tiled=True)
        level, stride = level + 1, 2 * stride
        doublings = DOUBLINGS[min(level, len(DOUBLINGS) - 1)]
        if stride < line:
            message, x, d, b = call(
                functools.partial(level_kernel, doublings),
                f"invert{level}",
                (d, b, terms, x),
                (square, square, square, tall),
            )
        else:
            (answer,) = call(
                functools.partial(end_kernel, doublings),
                "end",
                (info, d, b, terms, x),
                ((n, w),),
                scratch=(square,),
                scalars=True,
            )
    return answer[None]


def solution(mesh):
    placed = (P("line", None, None), P("line", None, None), P("line", None, "rhs"))
    return jax.shard_map(
        on_device, mesh=mesh, in_specs=placed, out_specs=P("line", None, "rhs"), check_vma=False
    )
```

```python
import functools
import jax
import jax.numpy as jnp
from jax import lax
from jax.experimental import pallas as pl
from jax.experimental.pallas import tpu as pltpu
from jax.sharding import PartitionSpec as P

F32 = jnp.float32
BF16 = jnp.bfloat16
BOTH = ("line", "rhs")
DOUBLINGS = (0, 2, 2, 3, 3, 2, 2, 0, 0)
STRETCH = (1.0, 1.5, 1.5, 1.5, 1.5, 1.5, 1.0, 1.0, 1.0)
RESIDUAL_MAX = 5.0e-3
SLOW_STEPS = 80


def split(x, terms):
    parts = []
    for i in range(terms):
        part = x.astype(BF16)
        parts.append(part)
        if i + 1 < terms:
            x = x - part.astype(F32)
    return parts


def one(a, b):
    return jnp.dot(a, b, preferred_element_type=F32)


def one_nt(a, b):
    return lax.dot_general(a, b, (((1,), (1,)), ((), ())), preferred_element_type=F32)


def product(a, b, dot=one):
    terms = len(a)
    total = None
    for order in range(terms - 1, -1, -1):
        for i in range(order + 1):
            term = dot(a[i], b[order - i])
            total = term if total is None else total + term
    return total


def unit(n):
    rows = lax.broadcasted_iota(jnp.int32, (n, n), 0)
    cols = lax.broadcasted_iota(jnp.int32, (n, n), 1)
    return (rows == cols).astype(F32)


def left_lanes(rows, half):
    return lax.broadcasted_iota(jnp.int32, (rows, 2 * half), 1) < half


def pack(x, tail, out):
    n = x.shape[0]
    h = n // 2
    corner = x[h:, h:]
    left = left_lanes(h, h // 2)
    out[:, :h] = x[:, :h]
    out[:h, h:] = jnp.where(left, corner, tail[:h])
    out[h:, h:] = jnp.where(left, pltpu.roll(corner, h // 2, 1), tail[h:])


def unpack(m):
    n = m.shape[0]
    h = n // 2
    tail = m[:, h:]
    left = left_lanes(h, h // 2)
    corner = jnp.where(left, tail[:h], pltpu.roll(tail[h:], h // 2, 1))
    low = m[h:, :h]
    top = jnp.concatenate([m[:h, :h], low.T], axis=1)
    bottom = jnp.concatenate([low, corner], axis=1)
    return jnp.concatenate([top, bottom], axis=0), tail


def invert(d, guess, doublings, x_ref):
    identity = unit(d.shape[0])
    d_parts = split(d, 3)
    guess_low = guess.astype(BF16)
    error = identity - one(d_parts[0], guess_low)
    power = error.astype(BF16)
    series = identity + error
    for _ in range(doublings):
        power = one(power, power).astype(BF16)
        series = series + one(series.astype(BF16), power)
    x = one(guess_low, series.astype(BF16))
    x_parts = split(x, 2)
    residual = identity - product(d_parts[:2], x_parts)
    x = x + one(x_parts[0], residual.astype(BF16))
    x_parts = split(x, 3)
    residual = identity - product(d_parts, x_parts)
    x_ref[...] = x + one(x_parts[0], residual.astype(BF16))
    size = jnp.sum(residual * residual)

    @pl.when(jnp.logical_not(size < RESIDUAL_MAX * RESIDUAL_MAX))
    def _():
        x_ref[...] = jnp.where(size < 0.25, x, guess)

        def keep_on(state):
            step, worst = state
            return jnp.logical_and(step < SLOW_STEPS, worst > 1.0e-6)

        def improve(state):
            step, _ = state
            x = x_ref[...]
            rest = identity - product(d_parts, split(x, 3))
            x = x + product(split(x, 3), split(rest, 3))
            x_ref[...] = 0.5 * (x + x.T)
            return step + 1, jnp.sum(rest * rest)

        lax.while_loop(keep_on, improve, (0, jnp.float32(1.0)))


def first_guess(d):
    identity = unit(d.shape[0])
    diagonal = jnp.sum(d * identity, axis=1, keepdims=True)
    reach = jnp.max(jnp.sum(jnp.abs(d), axis=1, keepdims=True) / diagonal)
    return identity * (jnp.minimum(1.0, 1.9 / reach) / diagonal)


def start_kernel(doublings, d_ref, b_ref, m_ref, x_ref, b_out):
    d = d_ref[...]
    invert(d, first_guess(d), doublings, x_ref)
    sides = b_ref[...]
    b = jnp.concatenate([jnp.zeros_like(sides), sides], axis=0).T
    b_out[...] = b
    x = x_ref[...]
    pack(x, product(split(x, 3), split(b, 3)), m_ref)


def reduce_rows(d_ref, b_ref, t_ref):
    n = d_ref.shape[0]
    first, first_tail = unpack(t_ref[:n])
    second, second_tail = unpack(t_ref[n:])
    b = b_ref[...] - first_tail - second_tail
    b = jnp.where(left_lanes(b.shape[0], b.shape[1] // 2), 0.0, b)
    return d_ref[...] - first - second, b


def level_kernel(doublings, stretch, d_ref, b_ref, t_ref, guess_ref, m_ref, x_ref, d_out, b_out):
    d, b = reduce_rows(d_ref, b_ref, t_ref)
    d_out[...] = d
    b_out[...] = b
    invert(d, stretch * guess_ref[...], doublings, x_ref)
    x = x_ref[...]
    pack(x, product(split(x, 3), split(b, 3)), m_ref)


def end_kernel(doublings, stretch, info, d_ref, b_ref, t_ref, guess_ref, out_ref, x_ref):
    d, b = reduce_rows(d_ref, b_ref, t_ref)
    invert(d, stretch * guess_ref[...], doublings, x_ref)
    answer = product(split(x_ref[...], 3), split(b, 3))
    w = out_ref.shape[1]
    answer = answer.T
    out_ref[0] = jnp.where(info[1] == 0, answer[2 * w : 3 * w], answer[3 * w :])


def transfer(c, info, m_ref, t_ref):
    n = c.shape[0]
    m = jnp.where(info[1] == 0, m_ref[n:], m_ref[:n])
    x, tail = unpack(m)
    c_parts = split(c, 3)
    z = product(c_parts, split(x, 3))
    pack(product(split(z, 3), c_parts, one_nt), product(c_parts, split(tail, 3)), t_ref)
    return z


def following(z, far):
    return -product(split(z, 3), split(far, 3))


def first_coupling_kernel(info, m_ref, low_ref, near_ref, far_ref, t_ref, c_out):
    below = info[1] == 0
    c = jnp.where(below, low_ref[...], near_ref[...].T)
    c = jnp.where(jnp.logical_and(below, info[0] == 0), 0.0, c)
    far = far_ref[...]
    far = jnp.where(below, far, far.T)
    far = jnp.where(jnp.logical_and(below, info[0] == 1), 0.0, far)
    c_out[...] = following(transfer(c, info, m_ref, t_ref), far)


def second_coupling_kernel(info, m_ref, c_ref, t_ref, z_out):
    z_out[...] = transfer(c_ref[...], info, m_ref, t_ref)


def coupling_kernel(info, m_ref, z_ref, far_ref, t_ref, z_out, c_out):
    c = following(z_ref[...], far_ref[...])
    c_out[...] = c
    z_out[...] = transfer(c, info, m_ref, t_ref)


def last_coupling_kernel(info, m_ref, z_ref, far_ref, t_ref):
    transfer(following(z_ref[...], far_ref[...]), info, m_ref, t_ref)


def call(kernel, name, operands, outs, scratch=(), scalars=False):
    specs = [pl.BlockSpec(memory_space=pltpu.VMEM)] * (len(operands) - int(scalars))
    if scalars:
        specs = [pl.BlockSpec(memory_space=pltpu.SMEM)] + specs
    shapes = [jax.ShapeDtypeStruct(shape, F32) for shape in outs]
    return pl.pallas_call(
        kernel,
        name=name,
        in_specs=specs,
        out_specs=[pl.BlockSpec(memory_space=pltpu.VMEM)] * len(outs),
        out_shape=shapes,
        scratch_shapes=[pltpu.VMEM(shape, F32) for shape in scratch],
        compiler_params=pltpu.CompilerParams(vmem_limit_bytes=40 * 2**20),
    )(*operands)


def pairs(line, stride):
    if 2 * stride < line:
        return [[2 * p, 2 * ((p - stride) % line) + 1] for p in range(line)]
    real = [[2 * p, 2 * (p - stride) + 1] for p in range(stride, line)]
    quarter = line // 4
    idle = [[2 * p, 2 * (p + (3 * quarter if p < quarter else quarter)) + 1] for p in range(stride)]
    return real + idle


def outward(line, stride, core0, core1):
    route = []
    for p in range(line):
        if core0 and p + core0 * stride < line:
            route.append((2 * p, 2 * (p + core0 * stride)))
        if p - core1 * stride >= 0:
            route.append((2 * p + 1, 2 * (p - core1 * stride) + 1))
    return route


def on_device(diag_blocks, lower_blocks, right_sides):
    d, low, b = diag_blocks[0], lower_blocks[0], right_sides[0]
    n, w = b.shape
    line = lax.axis_size("line")
    info = jnp.stack([lax.axis_index("line"), lax.axis_index("rhs")]).astype(jnp.int32)
    near = lax.ppermute(low, BOTH, outward(line, 1, 0, 1))
    far = lax.ppermute(low, BOTH, outward(line, 1, 1, 2))
    sides = lax.all_gather(b.T, "rhs", tiled=True)
    square, tall = (n, n), (n, 4 * w)
    level, stride = 0, 1
    message, x, b = call(
        functools.partial(start_kernel, DOUBLINGS[0]), "start", (d, sides), (square, square, tall)
    )
    while stride < line:
        both = lax.all_gather(message, BOTH, axis_index_groups=pairs(line, stride), tiled=True)
        if level == 0:
            term, c = call(
                first_coupling_kernel, "couple0", (info, both, low, near, far), (square, square), scalars=True
            )
        elif level == 1:
            term, z = call(second_coupling_kernel, "couple1", (info, both, c), (square, square), scalars=True)
        elif 2 * stride < line:
            term, z, c = call(
                coupling_kernel, f"couple{level}", (info, both, z, far), (square,) * 3, scalars=True
            )
        else:
            (term,) = call(
                last_coupling_kernel, f"couple{level}", (info, both, z, far), (square,), scalars=True
            )
        if level > 0 and 2 * stride < line:
            far = lax.ppermute(c, BOTH, outward(line, stride, 1, 1))
        terms = lax.all_gather(term, "rhs", tiled=True)
        level, stride = level + 1, 2 * stride
        place = min(level, len(DOUBLINGS) - 1)
        doublings, stretch = DOUBLINGS[place], STRETCH[place]
        if stride < line:
            message, x, d, b = call(
                functools.partial(level_kernel, doublings, stretch),
                f"invert{level}",
                (d, b, terms, x),
                (square, square, square, tall),
            )
        else:
            (answer,) = call(
                functools.partial(end_kernel, doublings, stretch),
                "end",
                (info, d, b, terms, x),
                ((1, w, n),),
                scratch=(square,),
                scalars=True,
            )
    return jnp.swapaxes(answer, 1, 2)


def solution(mesh):
    placed = (P("line", None, None), P("line", None, None), P("line", None, "rhs"))
    return jax.shard_map(
        on_device, mesh=mesh, in_specs=placed, out_specs=P("line", None, "rhs"), check_vma=False
    )
```

```python
import functools
import jax
import jax.numpy as jnp
from jax import lax
from jax.experimental import pallas as pl
from jax.experimental.pallas import tpu as pltpu
from jax.sharding import PartitionSpec as P

F32 = jnp.float32
BF16 = jnp.bfloat16
BOTH = ("line", "rhs")
DOUBLINGS = (0, 2, 2, 3, 3, 2, 2, 0, 0)
STRETCH = (1.0, 1.5, 1.5, 1.5, 1.5, 1.5, 1.0, 1.0, 1.0)
RESIDUAL_MAX = 5.0e-3
SLOW_STEPS = 80


def split(x, terms):
    parts = []
    for i in range(terms):
        part = x.astype(BF16)
        parts.append(part)
        if i + 1 < terms:
            x = x - part.astype(F32)
    return parts


def one(a, b):
    return jnp.dot(a, b, preferred_element_type=F32)


def one_nt(a, b):
    return lax.dot_general(a, b, (((1,), (1,)), ((), ())), preferred_element_type=F32)


def product(a, b, dot=one):
    terms = len(a)
    total = None
    for order in range(terms - 1, -1, -1):
        for i in range(order + 1):
            term = dot(a[i], b[order - i])
            total = term if total is None else total + term
    return total


def unit(n):
    rows = lax.broadcasted_iota(jnp.int32, (n, n), 0)
    cols = lax.broadcasted_iota(jnp.int32, (n, n), 1)
    return (rows == cols).astype(F32)


def left_lanes(rows, half):
    return lax.broadcasted_iota(jnp.int32, (rows, 2 * half), 1) < half


def pack(x, tail, out):
    h = x.shape[0] // 2
    q = h // 2
    left = left_lanes(q, q)
    out[:q] = jnp.where(left, x[:q, :h], pltpu.roll(x[h : h + q, h:], q, 1))
    out[q:h] = x[q:h, :h]
    out[h : 2 * h] = x[h:, :h]
    out[2 * h : 2 * h + q] = x[h + q :, h:]
    out[2 * h + q :] = jnp.where(left_lanes(h, q), pltpu.roll(tail[:h], q, 1), tail[h:])


def unpack(m):
    h = 2 * m.shape[0] // 7
    q = h // 2
    left = left_lanes(q, q)
    first, low, last, tail = m[:h], m[h : 2 * h], m[2 * h : 2 * h + q], m[2 * h + q :]
    upper = jnp.concatenate([jnp.where(left, first[:q], first.T[:q]), first[q:]], axis=0)
    mirrored = jnp.concatenate([last, last], axis=0).T[:q]
    corner = jnp.concatenate([jnp.where(left, pltpu.roll(first[:q], q, 1), mirrored), last], axis=0)
    top = jnp.concatenate([upper, low.T], axis=1)
    bottom = jnp.concatenate([low, corner], axis=1)
    return jnp.concatenate([top, bottom], axis=0), jnp.concatenate([pltpu.roll(tail, q, 1), tail], axis=0)


def invert(d, guess, b, doublings, x_ref, finish):
    identity = unit(d.shape[0])
    d_parts = split(d, 3)
    b_parts = split(b, 3)
    guess_low = guess.astype(BF16)
    error = identity - one(d_parts[0], guess_low)
    power = error.astype(BF16)
    series = identity + error
    for _ in range(doublings):
        power = one(power, power).astype(BF16)
        series = series + one(series.astype(BF16), power)
    x = one(guess_low, series.astype(BF16))
    x_parts = split(x, 2)
    residual = identity - product(d_parts[:2], x_parts)
    x = x + one(x_parts[0], residual.astype(BF16))
    x_parts = split(x, 3)
    residual = identity - product(d_parts, x_parts)
    rest = residual.astype(BF16)
    y = product(x_parts, b_parts) + one(x_parts[0], one(rest, b_parts[0]).astype(BF16))
    close = x + one(x_parts[0], rest)
    x_ref[...] = close
    finish(close, y)
    size = jnp.sum(residual * residual)

    @pl.when(jnp.logical_not(size < RESIDUAL_MAX * RESIDUAL_MAX))
    def _():
        x_ref[...] = jnp.where(size < 0.25, x, guess)

        def keep_on(state):
            step, worst = state
            return jnp.logical_and(step < SLOW_STEPS, worst > 1.0e-6)

        def improve(state):
            step, _ = state
            x = x_ref[...]
            rest = identity - product(d_parts, split(x, 3))
            x = x + product(split(x, 3), split(rest, 3))
            x_ref[...] = 0.5 * (x + x.T)
            return step + 1, jnp.sum(rest * rest)

        lax.while_loop(keep_on, improve, (0, jnp.float32(1.0)))
        finish(x_ref[...], product(split(x_ref[...], 3), b_parts))


def first_guess(d):
    identity = unit(d.shape[0])
    diagonal = jnp.sum(d * identity, axis=1, keepdims=True)
    reach = jnp.max(jnp.sum(jnp.abs(d), axis=1, keepdims=True) / diagonal)
    return identity * (jnp.minimum(1.0, 1.9 / reach) / diagonal)


def start_kernel(doublings, d_ref, b_ref, m_ref, x_ref, b_out):
    d = d_ref[...]
    sides = b_ref[...]
    b = jnp.concatenate([jnp.zeros_like(sides), sides], axis=0).T
    b_out[...] = b
    invert(d, first_guess(d), b, doublings, x_ref, lambda x, y: pack(x, y, m_ref))


def reduce_rows(d_ref, b_ref, t_ref):
    half = t_ref.shape[0] // 2
    term, tail = unpack(t_ref[:half] + t_ref[half:])
    b = b_ref[...] - tail
    b = jnp.where(left_lanes(b.shape[0], b.shape[1] // 2), 0.0, b)
    return d_ref[...] - term, b


def level_kernel(doublings, stretch, d_ref, b_ref, t_ref, guess_ref, m_ref, x_ref, d_out, b_out):
    d, b = reduce_rows(d_ref, b_ref, t_ref)
    d_out[...] = d
    b_out[...] = b
    invert(d, stretch * guess_ref[...], b, doublings, x_ref, lambda x, y: pack(x, y, m_ref))


def end_kernel(doublings, stretch, info, d_ref, b_ref, t_ref, guess_ref, out_ref, x_ref):
    d, b = reduce_rows(d_ref, b_ref, t_ref)
    w = out_ref.shape[1]

    def finish(_, y):
        y = y.T
        out_ref[0] = jnp.where(info[1] == 0, y[2 * w : 3 * w], y[3 * w :])

    invert(d, stretch * guess_ref[...], b, doublings, x_ref, finish)


def transfer(c, info, m_ref, t_ref):
    half = m_ref.shape[0] // 2
    m = jnp.where(info[1] == 0, m_ref[half:], m_ref[:half])
    x, tail = unpack(m)
    c_parts = split(c, 3)
    z = product(c_parts, split(x, 3))
    pack(product(split(z, 3), c_parts, one_nt), product(c_parts, split(tail, 3)), t_ref)
    return z


def following(z, far):
    return -product(split(z, 3), split(far, 3))


def first_coupling_kernel(info, m_ref, low_ref, near_ref, far_ref, t_ref, c_out):
    below = info[1] == 0
    c = jnp.where(below, low_ref[...], near_ref[...].T)
    c = jnp.where(jnp.logical_and(below, info[0] == 0), 0.0, c)
    far = far_ref[...]
    far = jnp.where(below, far, far.T)
    far = jnp.where(jnp.logical_and(below, info[0] == 1), 0.0, far)
    c_out[...] = following(transfer(c, info, m_ref, t_ref), far)


def second_coupling_kernel(info, m_ref, c_ref, t_ref, z_out):
    z_out[...] = transfer(c_ref[...], info, m_ref, t_ref)


def coupling_kernel(info, m_ref, z_ref, far_ref, t_ref, z_out, c_out):
    c = following(z_ref[...], far_ref[...])
    c_out[...] = c
    z_out[...] = transfer(c, info, m_ref, t_ref)


def last_coupling_kernel(info, m_ref, z_ref, far_ref, t_ref):
    transfer(following(z_ref[...], far_ref[...]), info, m_ref, t_ref)


def call(kernel, name, operands, outs, scratch=(), scalars=False):
    specs = [pl.BlockSpec(memory_space=pltpu.VMEM)] * (len(operands) - int(scalars))
    if scalars:
        specs = [pl.BlockSpec(memory_space=pltpu.SMEM)] + specs
    shapes = [jax.ShapeDtypeStruct(shape, F32) for shape in outs]
    return pl.pallas_call(
        kernel,
        name=name,
        in_specs=specs,
        out_specs=[pl.BlockSpec(memory_space=pltpu.VMEM)] * len(outs),
        out_shape=shapes,
        scratch_shapes=[pltpu.VMEM(shape, F32) for shape in scratch],
        compiler_params=pltpu.CompilerParams(vmem_limit_bytes=40 * 2**20),
    )(*operands)


def pairs(line, stride):
    if 2 * stride < line:
        return [[2 * p, 2 * ((p - stride) % line) + 1] for p in range(line)]
    real = [[2 * p, 2 * (p - stride) + 1] for p in range(stride, line)]
    quarter = line // 4
    idle = [[2 * p, 2 * (p + (3 * quarter if p < quarter else quarter)) + 1] for p in range(stride)]
    return real + idle


def outward(line, stride, core0, core1):
    route = []
    for p in range(line):
        if core0 and p + core0 * stride < line:
            route.append((2 * p, 2 * (p + core0 * stride)))
        if p - core1 * stride >= 0:
            route.append((2 * p + 1, 2 * (p - core1 * stride) + 1))
    return route


def on_device(diag_blocks, lower_blocks, right_sides):
    d, low, b = diag_blocks[0], lower_blocks[0], right_sides[0]
    n, w = b.shape
    line = lax.axis_size("line")
    info = jnp.stack([lax.axis_index("line"), lax.axis_index("rhs")]).astype(jnp.int32)
    near = lax.ppermute(low, BOTH, outward(line, 1, 0, 1))
    far = lax.ppermute(low, BOTH, outward(line, 1, 1, 2))
    sides = lax.all_gather(b.T, "rhs", tiled=True)
    square, tall, packed = (n, n), (n, 4 * w), (7 * n // 4, n // 2)
    level, stride = 0, 1
    message, x, b = call(
        functools.partial(start_kernel, DOUBLINGS[0]), "start", (d, sides), (packed, square, tall)
    )
    while stride < line:
        both = lax.all_gather(message, BOTH, axis_index_groups=pairs(line, stride), tiled=True)
        if level == 0:
            term, c = call(
                first_coupling_kernel, "couple0", (info, both, low, near, far), (packed, square), scalars=True
            )
        elif level == 1:
            term, z = call(second_coupling_kernel, "couple1", (info, both, c), (packed, square), scalars=True)
        elif 2 * stride < line:
            term, z, c = call(
                coupling_kernel, f"couple{level}", (info, both, z, far), (packed, square, square), scalars=True
            )
        else:
            (term,) = call(
                last_coupling_kernel, f"couple{level}", (info, both, z, far), (packed,), scalars=True
            )
        if level > 0 and 2 * stride < line:
            far = lax.ppermute(c, BOTH, outward(line, stride, 1, 1))
        terms = lax.all_gather(term, "rhs", tiled=True)
        level, stride = level + 1, 2 * stride
        place = min(level, len(DOUBLINGS) - 1)
        doublings, stretch = DOUBLINGS[place], STRETCH[place]
        if stride < line:
            message, x, d, b = call(
                functools.partial(level_kernel, doublings, stretch),
                f"invert{level}",
                (d, b, terms, x),
                (packed, square, square, tall),
            )
        else:
            (answer,) = call(
                functools.partial(end_kernel, doublings, stretch),
                "end",
                (info, d, b, terms, x),
                ((1, w, n),),
                scratch=(square,),
                scalars=True,
            )
    return jnp.swapaxes(answer, 1, 2)


def solution(mesh):
    placed = (P("line", None, None), P("line", None, None), P("line", None, "rhs"))
    return jax.shard_map(
        on_device, mesh=mesh, in_specs=placed, out_specs=P("line", None, "rhs"), check_vma=False
    )
```

```python
import functools
import jax
import jax.numpy as jnp
from jax import lax
from jax.experimental import pallas as pl
from jax.experimental.pallas import tpu as pltpu
from jax.sharding import PartitionSpec as P

F32 = jnp.float32
BF16 = jnp.bfloat16
BOTH = ("line", "rhs")
DOUBLINGS = (0, 2, 2, 3, 3, 2, 2, 0, 0)
STRETCH = (1.0, 1.5, 1.5, 1.5, 1.5, 1.5, 1.0, 1.0, 1.0)
RESIDUAL_MAX = 5.0e-3
SLOW_STEPS = 80
GATHERED = (0, 2)


def split(x, terms):
    parts = []
    for i in range(terms):
        part = x.astype(BF16)
        parts.append(part)
        if i + 1 < terms:
            x = x - part.astype(F32)
    return parts


def one(a, b):
    return jnp.dot(a, b, preferred_element_type=F32)


def one_nt(a, b):
    return lax.dot_general(a, b, (((1,), (1,)), ((), ())), preferred_element_type=F32)


def product(a, b, dot=one):
    terms = len(a)
    total = None
    for order in range(terms - 1, -1, -1):
        for i in range(order + 1):
            term = dot(a[i], b[order - i])
            total = term if total is None else total + term
    return total


def unit(n):
    rows = lax.broadcasted_iota(jnp.int32, (n, n), 0)
    cols = lax.broadcasted_iota(jnp.int32, (n, n), 1)
    return (rows == cols).astype(F32)


def left_lanes(rows, half):
    return lax.broadcasted_iota(jnp.int32, (rows, 2 * half), 1) < half


def pack(x, tail, out):
    h = x.shape[0] // 2
    q = h // 2
    left = left_lanes(q, q)
    out[:q] = jnp.where(left, x[:q, :h], pltpu.roll(x[h : h + q, h:], q, 1))
    out[q:h] = x[q:h, :h]
    out[h : 2 * h] = x[h:, :h]
    out[2 * h : 2 * h + q] = x[h + q :, h:]
    out[2 * h + q :] = jnp.where(left_lanes(h, q), pltpu.roll(tail[:h], q, 1), tail[h:])


def unpack(m):
    h = 2 * m.shape[0] // 7
    q = h // 2
    left = left_lanes(q, q)
    first, low, last, tail = m[:h], m[h : 2 * h], m[2 * h : 2 * h + q], m[2 * h + q :]
    upper = jnp.concatenate([jnp.where(left, first[:q], first.T[:q]), first[q:]], axis=0)
    mirrored = jnp.concatenate([last, last], axis=0).T[:q]
    corner = jnp.concatenate([jnp.where(left, pltpu.roll(first[:q], q, 1), mirrored), last], axis=0)
    top = jnp.concatenate([upper, low.T], axis=1)
    bottom = jnp.concatenate([low, corner], axis=1)
    return jnp.concatenate([top, bottom], axis=0), jnp.concatenate([pltpu.roll(tail, q, 1), tail], axis=0)


def invert(d, guess, b, doublings, x_ref, finish):
    identity = unit(d.shape[0])
    d_parts = split(d, 3)
    b_parts = split(b, 3)
    guess_low = guess.astype(BF16)
    error = identity - one(d_parts[0], guess_low)
    power = error.astype(BF16)
    series = identity + error
    for _ in range(doublings):
        power = one(power, power).astype(BF16)
        series = series + one(series.astype(BF16), power)
    x = one(guess_low, series.astype(BF16))
    x_parts = split(x, 2)
    residual = identity - product(d_parts[:2], x_parts)
    x = x + one(x_parts[0], residual.astype(BF16))
    x_parts = split(x, 3)
    residual = identity - product(d_parts, x_parts)
    rest = residual.astype(BF16)
    y = product(x_parts, b_parts) + one(x_parts[0], one(rest, b_parts[0]).astype(BF16))
    finish(x + one(x_parts[0], rest), y)
    size = jnp.sum(residual * residual)

    @pl.when(jnp.logical_not(size < RESIDUAL_MAX * RESIDUAL_MAX))
    def _():
        x_ref[...] = jnp.where(size < 0.25, x, guess)

        def keep_on(state):
            step, worst = state
            return jnp.logical_and(step < SLOW_STEPS, worst > 1.0e-6)

        def improve(state):
            step, _ = state
            x = x_ref[...]
            rest = identity - product(d_parts, split(x, 3))
            x = x + product(split(x, 3), split(rest, 3))
            x_ref[...] = 0.5 * (x + x.T)
            return step + 1, jnp.sum(rest * rest)

        lax.while_loop(keep_on, improve, (0, jnp.float32(1.0)))
        finish(x_ref[...], product(split(x_ref[...], 3), b_parts))


def keep(x_ref, m_ref):
    def finish(x, y):
        x_ref[...] = x
        pack(x, y, m_ref)

    return finish


def first_guess(d):
    identity = unit(d.shape[0])
    diagonal = jnp.sum(d * identity, axis=1, keepdims=True)
    reach = jnp.max(jnp.sum(jnp.abs(d), axis=1, keepdims=True) / diagonal)
    return identity * (jnp.minimum(1.0, 1.9 / reach) / diagonal)


def start_kernel(doublings, d_ref, b_ref, m_ref, x_ref, b_out):
    d = d_ref[...]
    sides = b_ref[...]
    b = jnp.concatenate([jnp.zeros_like(sides), sides], axis=0).T
    b_out[...] = b
    invert(d, first_guess(d), b, doublings, x_ref, keep(x_ref, m_ref))


def reduce_rows(d_ref, b_ref, t_ref):
    half = t_ref.shape[0] // 2
    term, tail = unpack(t_ref[:half] + t_ref[half:])
    b = b_ref[...] - tail
    b = jnp.where(left_lanes(b.shape[0], b.shape[1] // 2), 0.0, b)
    return d_ref[...] - term, b


def level_kernel(doublings, stretch, d_ref, b_ref, t_ref, guess_ref, m_ref, x_ref, d_out, b_out):
    d, b = reduce_rows(d_ref, b_ref, t_ref)
    d_out[...] = d
    b_out[...] = b
    invert(d, stretch * guess_ref[...], b, doublings, x_ref, keep(x_ref, m_ref))


def end_kernel(doublings, stretch, info, d_ref, b_ref, t_ref, guess_ref, out_ref, x_ref):
    d, b = reduce_rows(d_ref, b_ref, t_ref)
    w = out_ref.shape[1]

    def finish(_, y):
        y = y.T
        out_ref[0] = jnp.where(info[1] == 0, y[2 * w : 3 * w], y[3 * w :])

    invert(d, stretch * guess_ref[...], b, doublings, x_ref, finish)


def transfer(c, m, t_ref):
    x, tail = unpack(m)
    c_parts = split(c, 3)
    z = product(c_parts, split(x, 3))
    pack(product(split(z, 3), c_parts, one_nt), product(c_parts, split(tail, 3)), t_ref)
    return z


def received(info, m_ref):
    return m_ref[...] if len(m_ref.shape) == 2 else jnp.where(info[1] == 0, m_ref[1], m_ref[0])


def following(z, far):
    return -product(split(z, 3), split(far, 3))


def first_coupling_kernel(info, m_ref, low_ref, near_ref, far_ref, t_ref, c_out):
    below = info[1] == 0
    c = jnp.where(below, low_ref[...], near_ref[...].T)
    c = jnp.where(jnp.logical_and(below, info[0] == 0), 0.0, c)
    far = far_ref[...]
    far = jnp.where(below, far, far.T)
    far = jnp.where(jnp.logical_and(below, info[0] == 1), 0.0, far)
    c_out[...] = following(transfer(c, received(info, m_ref), t_ref), far)


def coupling_kernel(info, m_ref, c_ref, t_ref, z_out):
    z_out[...] = transfer(c_ref[...], received(info, m_ref), t_ref)


def following_kernel(z_ref, far_ref, c_out):
    c_out[...] = following(z_ref[...], far_ref[...])


def last_coupling_kernel(m_ref, c_ref, t_ref):
    transfer(c_ref[...], m_ref[...], t_ref)


def call(kernel, name, operands, outs, scratch=(), scalars=False):
    specs = [pl.BlockSpec(memory_space=pltpu.VMEM)] * (len(operands) - int(scalars))
    if scalars:
        specs = [pl.BlockSpec(memory_space=pltpu.SMEM)] + specs
    shapes = [jax.ShapeDtypeStruct(shape, F32) for shape in outs]
    return pl.pallas_call(
        kernel,
        name=name,
        in_specs=specs,
        out_specs=[pl.BlockSpec(memory_space=pltpu.VMEM)] * len(outs),
        out_shape=shapes,
        scratch_shapes=[pltpu.VMEM(shape, F32) for shape in scratch],
        compiler_params=pltpu.CompilerParams(vmem_limit_bytes=40 * 2**20),
    )(*operands)


def pairs(line, stride):
    return [[2 * p, 2 * ((p - stride) % line) + 1] for p in range(line)]


def swapped(line, stride):
    both = [(2 * p, 2 * (p - stride) + 1) for p in range(stride, line)]
    return both + [(b, a) for a, b in both]


def outward(line, stride, core0, core1):
    route = []
    for p in range(line):
        if core0 and p + core0 * stride < line:
            route.append((2 * p, 2 * (p + core0 * stride)))
        if p - core1 * stride >= 0:
            route.append((2 * p + 1, 2 * (p - core1 * stride) + 1))
    return route


def on_device(diag_blocks, lower_blocks, right_sides):
    d, low, b = diag_blocks[0], lower_blocks[0], right_sides[0]
    n, w = b.shape
    line = lax.axis_size("line")
    info = jnp.stack([lax.axis_index("line"), lax.axis_index("rhs")]).astype(jnp.int32)
    near = lax.ppermute(low, BOTH, outward(line, 1, 0, 1))
    far = lax.ppermute(low, BOTH, outward(line, 1, 1, 2))
    sides = lax.all_gather(b.T, "rhs", tiled=True)
    square, tall, packed = (n, n), (n, 4 * w), (7 * n // 4, n // 2)
    level, stride = 0, 1
    message, x, b = call(
        functools.partial(start_kernel, DOUBLINGS[0]), "start", (d, sides), (packed, square, tall)
    )
    while stride < line:
        if level in GATHERED:
            near_m = lax.all_gather(message, BOTH, axis_index_groups=pairs(line, stride))
        else:
            near_m = lax.ppermute(message, BOTH, swapped(line, stride))
        if level in GATHERED and level > 1:
            near_m, z = lax.optimization_barrier((near_m, z))
        if level > 1:
            (c,) = call(following_kernel, f"follow{level}", (z, far), (square,))
        if level == 0:
            term, c = call(
                first_coupling_kernel, "couple0", (info, near_m, low, near, far), (packed, square), scalars=True
            )
        elif 2 * stride < line:
            term, z = call(coupling_kernel, f"couple{level}", (info, near_m, c), (packed, square), scalars=True)
            far = lax.ppermute(c, BOTH, outward(line, stride, 1, 1))
        else:
            (term,) = call(last_coupling_kernel, f"couple{level}", (near_m, c), (packed,))
        terms = lax.all_gather(term, "rhs", tiled=True)
        level, stride = level + 1, 2 * stride
        place = min(level, len(DOUBLINGS) - 1)
        doublings, stretch = DOUBLINGS[place], STRETCH[place]
        if stride < line:
            message, x, d, b = call(
                functools.partial(level_kernel, doublings, stretch),
                f"invert{level}",
                (d, b, terms, x),
                (packed, square, square, tall),
            )
        else:
            (answer,) = call(
                functools.partial(end_kernel, doublings, stretch),
                "end",
                (info, d, b, terms, x),
                ((1, w, n),),
                scratch=(square,),
                scalars=True,
            )
    return jnp.swapaxes(answer, 1, 2)


def solution(mesh):
    placed = (P("line", None, None), P("line", None, None), P("line", None, "rhs"))
    return jax.shard_map(
        on_device, mesh=mesh, in_specs=placed, out_specs=P("line", None, "rhs"), check_vma=False
    )
```

```python
import functools
import jax
import jax.numpy as jnp
from jax import lax
from jax.experimental import pallas as pl
from jax.experimental.pallas import tpu as pltpu
from jax.sharding import PartitionSpec as P

F32 = jnp.float32
BF16 = jnp.bfloat16
BOTH = ("line", "rhs")
DOUBLINGS = (0, 2, 2, 3, 3, 2, 2, 0, 0)
STRETCH = (1.0, 1.5, 1.5, 1.5, 1.5, 1.5, 1.0, 1.0, 1.0)
RESIDUAL_MAX = 5.0e-3
SLOW_STEPS = 80
HELD = (2,)


def split(x, terms):
    parts = []
    for i in range(terms):
        part = x.astype(BF16)
        parts.append(part)
        if i + 1 < terms:
            x = x - part.astype(F32)
    return parts


def one(a, b):
    return jnp.dot(a, b, preferred_element_type=F32)


def one_nt(a, b):
    return lax.dot_general(a, b, (((1,), (1,)), ((), ())), preferred_element_type=F32)


def product(a, b, dot=one):
    terms = len(a)
    total = None
    for order in range(terms - 1, -1, -1):
        for i in range(order + 1):
            term = dot(a[i], b[order - i])
            total = term if total is None else total + term
    return total


def unit(n):
    rows = lax.broadcasted_iota(jnp.int32, (n, n), 0)
    cols = lax.broadcasted_iota(jnp.int32, (n, n), 1)
    return (rows == cols).astype(F32)


def left_lanes(rows, half):
    return lax.broadcasted_iota(jnp.int32, (rows, 2 * half), 1) < half


def pack(x, tail, out):
    h = x.shape[0] // 2
    q = h // 2
    left = left_lanes(q, q)
    out[:q] = jnp.where(left, x[:q, :h], pltpu.roll(x[h : h + q, h:], q, 1))
    out[q:h] = x[q:h, :h]
    out[h : 2 * h] = x[h:, :h]
    out[2 * h : 2 * h + q] = x[h + q :, h:]
    out[2 * h + q :] = jnp.where(left_lanes(h, q), pltpu.roll(tail[:h], q, 1), tail[h:])


def unpack(m):
    h = 2 * m.shape[0] // 7
    q = h // 2
    left = left_lanes(q, q)
    first, low, last, tail = m[:h], m[h : 2 * h], m[2 * h : 2 * h + q], m[2 * h + q :]
    upper = jnp.concatenate([jnp.where(left, first[:q], first.T[:q]), first[q:]], axis=0)
    mirrored = jnp.concatenate([last, last], axis=0).T[:q]
    corner = jnp.concatenate([jnp.where(left, pltpu.roll(first[:q], q, 1), mirrored), last], axis=0)
    top = jnp.concatenate([upper, low.T], axis=1)
    bottom = jnp.concatenate([low, corner], axis=1)
    return jnp.concatenate([top, bottom], axis=0), jnp.concatenate([pltpu.roll(tail, q, 1), tail], axis=0)


def invert(d, guess, b, doublings, x_ref, finish):
    identity = unit(d.shape[0])
    d_parts = split(d, 3)
    b_parts = split(b, 3)
    guess_low = guess.astype(BF16)
    error = identity - one(d_parts[0], guess_low)
    power = error.astype(BF16)
    series = identity + error
    for _ in range(doublings):
        power = one(power, power).astype(BF16)
        series = series + one(series.astype(BF16), power)
    x = one(guess_low, series.astype(BF16))
    x_parts = split(x, 2)
    residual = identity - product(d_parts[:2], x_parts)
    x = x + one(x_parts[0], residual.astype(BF16))
    x_parts = split(x, 3)
    residual = identity - product(d_parts, x_parts)
    rest = residual.astype(BF16)
    y = product(x_parts, b_parts) + one(x_parts[0], one(rest, b_parts[0]).astype(BF16))
    finish(x + one(x_parts[0], rest), y)
    size = jnp.sum(residual * residual)

    @pl.when(jnp.logical_not(size < RESIDUAL_MAX * RESIDUAL_MAX))
    def _():
        x_ref[...] = jnp.where(size < 0.25, x, guess)

        def keep_on(state):
            step, worst = state
            return jnp.logical_and(step < SLOW_STEPS, worst > 1.0e-6)

        def improve(state):
            step, _ = state
            x = x_ref[...]
            rest = identity - product(d_parts, split(x, 3))
            x = x + product(split(x, 3), split(rest, 3))
            x_ref[...] = 0.5 * (x + x.T)
            return step + 1, jnp.sum(rest * rest)

        lax.while_loop(keep_on, improve, (0, jnp.float32(1.0)))
        finish(x_ref[...], product(split(x_ref[...], 3), b_parts))


def keep(x_ref, m_ref):
    def finish(x, y):
        x_ref[...] = x
        pack(x, y, m_ref)

    return finish


def first_guess(d):
    identity = unit(d.shape[0])
    diagonal = jnp.sum(d * identity, axis=1, keepdims=True)
    reach = jnp.max(jnp.sum(jnp.abs(d), axis=1, keepdims=True) / diagonal)
    return identity * (jnp.minimum(1.0, 1.9 / reach) / diagonal)


def start_kernel(doublings, d_ref, b_ref, m_ref, x_ref, b_out):
    d = d_ref[...]
    sides = b_ref[...]
    b = jnp.concatenate([jnp.zeros_like(sides), sides], axis=0).T
    b_out[...] = b
    invert(d, first_guess(d), b, doublings, x_ref, keep(x_ref, m_ref))


def reduce_rows(d_ref, b_ref, t_ref):
    half = t_ref.shape[0] // 2
    term, tail = unpack(t_ref[:half] + t_ref[half:])
    b = b_ref[...] - tail
    b = jnp.where(left_lanes(b.shape[0], b.shape[1] // 2), 0.0, b)
    return d_ref[...] - term, b


def level_kernel(doublings, stretch, d_ref, b_ref, t_ref, guess_ref, m_ref, x_ref, d_out, b_out):
    d, b = reduce_rows(d_ref, b_ref, t_ref)
    d_out[...] = d
    b_out[...] = b
    invert(d, stretch * guess_ref[...], b, doublings, x_ref, keep(x_ref, m_ref))


def end_kernel(doublings, stretch, info, d_ref, b_ref, t_ref, guess_ref, out_ref, x_ref):
    d, b = reduce_rows(d_ref, b_ref, t_ref)
    w = out_ref.shape[1]

    def finish(_, y):
        y = y.T
        out_ref[0] = jnp.where(info[1] == 0, y[2 * w : 3 * w], y[3 * w :])

    invert(d, stretch * guess_ref[...], b, doublings, x_ref, finish)


def transfer(c, m, t_ref):
    x, tail = unpack(m)
    c_parts = split(c, 3)
    z = product(c_parts, split(x, 3))
    pack(product(split(z, 3), c_parts, one_nt), product(c_parts, split(tail, 3)), t_ref)
    return z


def following(z, far):
    return -product(split(z, 3), split(far, 3))


def first_coupling_kernel(info, m_ref, low_ref, near_ref, far_ref, t_ref, c_out):
    below = info[1] == 0
    c = jnp.where(below, low_ref[...], near_ref[...].T)
    c = jnp.where(jnp.logical_and(below, info[0] == 0), 0.0, c)
    far = far_ref[...]
    far = jnp.where(below, far, far.T)
    far = jnp.where(jnp.logical_and(below, info[0] == 1), 0.0, far)
    c_out[...] = following(transfer(c, m_ref[...], t_ref), far)


def coupling_kernel(m_ref, c_ref, t_ref, z_out):
    z_out[...] = transfer(c_ref[...], m_ref[...], t_ref)


def following_kernel(z_ref, far_ref, c_out):
    c_out[...] = following(z_ref[...], far_ref[...])


def last_coupling_kernel(m_ref, c_ref, t_ref):
    transfer(c_ref[...], m_ref[...], t_ref)


def call(kernel, name, operands, outs, scratch=(), scalars=False):
    specs = [pl.BlockSpec(memory_space=pltpu.VMEM)] * (len(operands) - int(scalars))
    if scalars:
        specs = [pl.BlockSpec(memory_space=pltpu.SMEM)] + specs
    shapes = [jax.ShapeDtypeStruct(shape, F32) for shape in outs]
    return pl.pallas_call(
        kernel,
        name=name,
        in_specs=specs,
        out_specs=[pl.BlockSpec(memory_space=pltpu.VMEM)] * len(outs),
        out_shape=shapes,
        scratch_shapes=[pltpu.VMEM(shape, F32) for shape in scratch],
        compiler_params=pltpu.CompilerParams(vmem_limit_bytes=40 * 2**20),
    )(*operands)


def swapped(line, stride):
    both = [(2 * p, 2 * (p - stride) + 1) for p in range(stride, line)]
    return both + [(b, a) for a, b in both]


def outward(line, stride, core0, core1):
    route = []
    for p in range(line):
        if core0 and p + core0 * stride < line:
            route.append((2 * p, 2 * (p + core0 * stride)))
        if p - core1 * stride >= 0:
            route.append((2 * p + 1, 2 * (p - core1 * stride) + 1))
    return route


def on_device(diag_blocks, lower_blocks, right_sides):
    d, low, b = diag_blocks[0], lower_blocks[0], right_sides[0]
    n, w = b.shape
    line = lax.axis_size("line")
    info = jnp.stack([lax.axis_index("line"), lax.axis_index("rhs")]).astype(jnp.int32)
    near = lax.ppermute(low, BOTH, outward(line, 1, 0, 1))
    far = lax.ppermute(low, BOTH, outward(line, 1, 1, 2))
    sides = lax.all_gather(b.T, "rhs", tiled=True)
    square, tall, packed = (n, n), (n, 4 * w), (7 * n // 4, n // 2)
    level, stride = 0, 1
    message, x, b = call(
        functools.partial(start_kernel, DOUBLINGS[0]), "start", (d, sides), (packed, square, tall)
    )
    while stride < line:
        near_m = lax.ppermute(message, BOTH, swapped(line, stride))
        if level > 1:
            (c,) = call(following_kernel, f"follow{level}", (z, far), (square,))
        if level in HELD:
            near_m, c = lax.optimization_barrier((near_m, c))
        if level == 0:
            term, c = call(
                first_coupling_kernel, "couple0", (info, near_m, low, near, far), (packed, square), scalars=True
            )
        elif 2 * stride < line:
            term, z = call(coupling_kernel, f"couple{level}", (near_m, c), (packed, square))
            far = lax.ppermute(c, BOTH, outward(line, stride, 1, 1))
        else:
            (term,) = call(last_coupling_kernel, f"couple{level}", (near_m, c), (packed,))
        terms = lax.all_gather(term, "rhs", tiled=True)
        level, stride = level + 1, 2 * stride
        place = min(level, len(DOUBLINGS) - 1)
        doublings, stretch = DOUBLINGS[place], STRETCH[place]
        if stride < line:
            message, x, d, b = call(
                functools.partial(level_kernel, doublings, stretch),
                f"invert{level}",
                (d, b, terms, x),
                (packed, square, square, tall),
            )
        else:
            (answer,) = call(
                functools.partial(end_kernel, doublings, stretch),
                "end",
                (info, d, b, terms, x),
                ((1, w, n),),
                scratch=(square,),
                scalars=True,
            )
    return jnp.swapaxes(answer, 1, 2)


def solution(mesh):
    placed = (P("line", None, None), P("line", None, None), P("line", None, "rhs"))
    return jax.shard_map(
        on_device, mesh=mesh, in_specs=placed, out_specs=P("line", None, "rhs"), check_vma=False
    )
```

```python
import functools
import jax
import jax.numpy as jnp
from jax import lax
from jax.experimental import pallas as pl
from jax.experimental.pallas import tpu as pltpu
from jax.sharding import PartitionSpec as P

F32 = jnp.float32
BF16 = jnp.bfloat16
BOTH = ("line", "rhs")
DOUBLINGS = (0, 2, 2, 3, 3, 2, 2, 0, 0)
STRETCH = (1.0, 1.5, 1.5, 1.5, 1.5, 1.5, 1.0, 1.0, 1.0)
RESIDUAL_MAX = 5.0e-3
SLOW_STEPS = 80
GATHERED = (0,)
HELD = (2,)


def split(x, terms):
    parts = []
    for i in range(terms):
        part = x.astype(BF16)
        parts.append(part)
        if i + 1 < terms:
            x = x - part.astype(F32)
    return parts


def one(a, b):
    return jnp.dot(a, b, preferred_element_type=F32)


def one_nt(a, b):
    return lax.dot_general(a, b, (((1,), (1,)), ((), ())), preferred_element_type=F32)


def product(a, b, dot=one):
    terms = len(a)
    total = None
    for order in range(terms - 1, -1, -1):
        for i in range(order + 1):
            term = dot(a[i], b[order - i])
            total = term if total is None else total + term
    return total


def unit(n):
    rows = lax.broadcasted_iota(jnp.int32, (n, n), 0)
    cols = lax.broadcasted_iota(jnp.int32, (n, n), 1)
    return (rows == cols).astype(F32)


def left_lanes(rows, half):
    return lax.broadcasted_iota(jnp.int32, (rows, 2 * half), 1) < half


def pack(x, tail, out):
    h = x.shape[0] // 2
    q = h // 2
    left = left_lanes(q, q)
    out[:q] = jnp.where(left, x[:q, :h], pltpu.roll(x[h : h + q, h:], q, 1))
    out[q:h] = x[q:h, :h]
    out[h : 2 * h] = x[h:, :h]
    out[2 * h : 2 * h + q] = x[h + q :, h:]
    out[2 * h + q :] = jnp.where(left_lanes(h, q), pltpu.roll(tail[:h], q, 1), tail[h:])


def unpack(m):
    h = 2 * m.shape[0] // 7
    q = h // 2
    left = left_lanes(q, q)
    first, low, last, tail = m[:h], m[h : 2 * h], m[2 * h : 2 * h + q], m[2 * h + q :]
    upper = jnp.concatenate([jnp.where(left, first[:q], first.T[:q]), first[q:]], axis=0)
    mirrored = jnp.concatenate([last, last], axis=0).T[:q]
    corner = jnp.concatenate([jnp.where(left, pltpu.roll(first[:q], q, 1), mirrored), last], axis=0)
    top = jnp.concatenate([upper, low.T], axis=1)
    bottom = jnp.concatenate([low, corner], axis=1)
    return jnp.concatenate([top, bottom], axis=0), jnp.concatenate([pltpu.roll(tail, q, 1), tail], axis=0)


def invert(d, guess, b, doublings, x_ref, finish):
    identity = unit(d.shape[0])
    d_parts = split(d, 3)
    b_parts = split(b, 3)
    guess_low = guess.astype(BF16)
    error = identity - one(d_parts[0], guess_low)
    power = error.astype(BF16)
    series = identity + error
    for _ in range(doublings):
        power = one(power, power).astype(BF16)
        series = series + one(series.astype(BF16), power)
    x = one(guess_low, series.astype(BF16))
    x_parts = split(x, 2)
    residual = identity - product(d_parts[:2], x_parts)
    x = x + one(x_parts[0], residual.astype(BF16))
    x_parts = split(x, 3)
    residual = identity - product(d_parts, x_parts)
    rest = residual.astype(BF16)
    y = product(x_parts, b_parts) + one(x_parts[0], one(rest, b_parts[0]).astype(BF16))
    finish(x + one(x_parts[0], rest), y)
    size = jnp.sum(residual * residual)

    @pl.when(jnp.logical_not(size < RESIDUAL_MAX * RESIDUAL_MAX))
    def _():
        x_ref[...] = jnp.where(size < 0.25, x, guess)

        def keep_on(state):
            step, worst = state
            return jnp.logical_and(step < SLOW_STEPS, worst > 1.0e-6)

        def improve(state):
            step, _ = state
            x = x_ref[...]
            rest = identity - product(d_parts, split(x, 3))
            x = x + product(split(x, 3), split(rest, 3))
            x_ref[...] = 0.5 * (x + x.T)
            return step + 1, jnp.sum(rest * rest)

        lax.while_loop(keep_on, improve, (0, jnp.float32(1.0)))
        finish(x_ref[...], product(split(x_ref[...], 3), b_parts))


def keep(x_ref, m_ref):
    def finish(x, y):
        x_ref[...] = x
        pack(x, y, m_ref)

    return finish


def first_guess(d):
    identity = unit(d.shape[0])
    diagonal = jnp.sum(d * identity, axis=1, keepdims=True)
    reach = jnp.max(jnp.sum(jnp.abs(d), axis=1, keepdims=True) / diagonal)
    return identity * (jnp.minimum(1.0, 1.9 / reach) / diagonal)


def start_kernel(doublings, d_ref, b_ref, m_ref, x_ref, b_out):
    d = d_ref[...]
    sides = b_ref[...]
    b = jnp.concatenate([jnp.zeros_like(sides), sides], axis=0).T
    b_out[...] = b
    invert(d, first_guess(d), b, doublings, x_ref, keep(x_ref, m_ref))


def reduce_rows(d_ref, b_ref, t_ref):
    half = t_ref.shape[0] // 2
    term, tail = unpack(t_ref[:half] + t_ref[half:])
    b = b_ref[...] - tail
    b = jnp.where(left_lanes(b.shape[0], b.shape[1] // 2), 0.0, b)
    return d_ref[...] - term, b


def level_kernel(doublings, stretch, d_ref, b_ref, t_ref, guess_ref, m_ref, x_ref, d_out, b_out):
    d, b = reduce_rows(d_ref, b_ref, t_ref)
    d_out[...] = d
    b_out[...] = b
    invert(d, stretch * guess_ref[...], b, doublings, x_ref, keep(x_ref, m_ref))


def end_kernel(doublings, stretch, info, d_ref, b_ref, t_ref, guess_ref, out_ref, x_ref):
    d, b = reduce_rows(d_ref, b_ref, t_ref)
    w = out_ref.shape[1]

    def finish(_, y):
        y = y.T
        out_ref[0] = jnp.where(info[1] == 0, y[2 * w : 3 * w], y[3 * w :])

    invert(d, stretch * guess_ref[...], b, doublings, x_ref, finish)


def transfer(c, m, t_ref):
    x, tail = unpack(m)
    c_parts = split(c, 3)
    z = product(c_parts, split(x, 3))
    pack(product(split(z, 3), c_parts, one_nt), product(c_parts, split(tail, 3)), t_ref)
    return z


def received(info, m_ref):
    return m_ref[...] if len(m_ref.shape) == 2 else jnp.where(info[1] == 0, m_ref[1], m_ref[0])


def following(z, far):
    return -product(split(z, 3), split(far, 3))


def first_coupling_kernel(info, m_ref, low_ref, near_ref, far_ref, t_ref, c_out):
    below = info[1] == 0
    c = jnp.where(below, low_ref[...], near_ref[...].T)
    c = jnp.where(jnp.logical_and(below, info[0] == 0), 0.0, c)
    far = far_ref[...]
    far = jnp.where(below, far, far.T)
    far = jnp.where(jnp.logical_and(below, info[0] == 1), 0.0, far)
    c_out[...] = following(transfer(c, received(info, m_ref), t_ref), far)


def coupling_kernel(m_ref, c_ref, t_ref, z_out):
    z_out[...] = transfer(c_ref[...], m_ref[...], t_ref)


def following_kernel(z_ref, far_ref, c_out):
    c_out[...] = following(z_ref[...], far_ref[...])


def last_coupling_kernel(m_ref, c_ref, t_ref):
    transfer(c_ref[...], m_ref[...], t_ref)


def call(kernel, name, operands, outs, scratch=(), scalars=False):
    specs = [pl.BlockSpec(memory_space=pltpu.VMEM)] * (len(operands) - int(scalars))
    if scalars:
        specs = [pl.BlockSpec(memory_space=pltpu.SMEM)] + specs
    shapes = [jax.ShapeDtypeStruct(shape, F32) for shape in outs]
    return pl.pallas_call(
        kernel,
        name=name,
        in_specs=specs,
        out_specs=[pl.BlockSpec(memory_space=pltpu.VMEM)] * len(outs),
        out_shape=shapes,
        scratch_shapes=[pltpu.VMEM(shape, F32) for shape in scratch],
        compiler_params=pltpu.CompilerParams(vmem_limit_bytes=40 * 2**20),
    )(*operands)


def pairs(line, stride):
    return [[2 * p, 2 * ((p - stride) % line) + 1] for p in range(line)]


def swapped(line, stride):
    both = [(2 * p, 2 * (p - stride) + 1) for p in range(stride, line)]
    return both + [(b, a) for a, b in both]


def outward(line, stride, core0, core1):
    route = []
    for p in range(line):
        if core0 and p + core0 * stride < line:
            route.append((2 * p, 2 * (p + core0 * stride)))
        if p - core1 * stride >= 0:
            route.append((2 * p + 1, 2 * (p - core1 * stride) + 1))
    return route


def on_device(diag_blocks, lower_blocks, right_sides):
    d, low, b = diag_blocks[0], lower_blocks[0], right_sides[0]
    n, w = b.shape
    line = lax.axis_size("line")
    info = jnp.stack([lax.axis_index("line"), lax.axis_index("rhs")]).astype(jnp.int32)
    near = lax.ppermute(low, BOTH, outward(line, 1, 0, 1))
    far = lax.ppermute(low, BOTH, outward(line, 1, 1, 2))
    sides = lax.all_gather(b.T, "rhs", tiled=True)
    square, tall, packed = (n, n), (n, 4 * w), (7 * n // 4, n // 2)
    level, stride = 0, 1
    message, x, b = call(
        functools.partial(start_kernel, DOUBLINGS[0]), "start", (d, sides), (packed, square, tall)
    )
    while stride < line:
        if level in GATHERED:
            near_m = lax.all_gather(message, BOTH, axis_index_groups=pairs(line, stride))
        else:
            near_m = lax.ppermute(message, BOTH, swapped(line, stride))
        if level > 1:
            (c,) = call(following_kernel, f"follow{level}", (z, far), (square,))
        if level in HELD:
            near_m, c = lax.optimization_barrier((near_m, c))
        if level == 0:
            term, c = call(
                first_coupling_kernel, "couple0", (info, near_m, low, near, far), (packed, square), scalars=True
            )
        elif 2 * stride < line:
            term, z = call(coupling_kernel, f"couple{level}", (near_m, c), (packed, square))
            far = lax.ppermute(c, BOTH, outward(line, stride, 1, 1))
        else:
            (term,) = call(last_coupling_kernel, f"couple{level}", (near_m, c), (packed,))
        terms = lax.all_gather(term, "rhs", tiled=True)
        level, stride = level + 1, 2 * stride
        place = min(level, len(DOUBLINGS) - 1)
        doublings, stretch = DOUBLINGS[place], STRETCH[place]
        if stride < line:
            message, x, d, b = call(
                functools.partial(level_kernel, doublings, stretch),
                f"invert{level}",
                (d, b, terms, x),
                (packed, square, square, tall),
            )
        else:
            (answer,) = call(
                functools.partial(end_kernel, doublings, stretch),
                "end",
                (info, d, b, terms, x),
                ((1, w, n),),
                scratch=(square,),
                scalars=True,
            )
    return jnp.swapaxes(answer, 1, 2)


def solution(mesh):
    placed = (P("line", None, None), P("line", None, None), P("line", None, "rhs"))
    return jax.shard_map(
        on_device, mesh=mesh, in_specs=placed, out_specs=P("line", None, "rhs"), check_vma=False
    )
```

```python
import functools
import jax
import jax.numpy as jnp
from jax import lax
from jax.experimental import pallas as pl
from jax.experimental.pallas import tpu as pltpu
from jax.sharding import PartitionSpec as P

F32 = jnp.float32
BF16 = jnp.bfloat16
BOTH = ("line", "rhs")
DOUBLINGS = (0, 2, 2, 3, 3, 2, 2, 0, 0)
STRETCH = (1.0, 1.5, 1.5, 1.5, 1.5, 1.5, 1.0, 1.0, 1.0)
RESIDUAL_MAX = 5.0e-3
SLOW_STEPS = 80
GATHERED = (0, 1)
HELD = (2,)


def split(x, terms):
    parts = []
    for i in range(terms):
        part = x.astype(BF16)
        parts.append(part)
        if i + 1 < terms:
            x = x - part.astype(F32)
    return parts


def one(a, b):
    return jnp.dot(a, b, preferred_element_type=F32)


def one_nt(a, b):
    return lax.dot_general(a, b, (((1,), (1,)), ((), ())), preferred_element_type=F32)


def product(a, b, dot=one):
    terms = len(a)
    total = None
    for order in range(terms - 1, -1, -1):
        for i in range(order + 1):
            term = dot(a[i], b[order - i])
            total = term if total is None else total + term
    return total


def unit(n):
    rows = lax.broadcasted_iota(jnp.int32, (n, n), 0)
    cols = lax.broadcasted_iota(jnp.int32, (n, n), 1)
    return (rows == cols).astype(F32)


def left_lanes(rows, half):
    return lax.broadcasted_iota(jnp.int32, (rows, 2 * half), 1) < half


def pack(x, tail, out):
    h = x.shape[0] // 2
    q = h // 2
    left = left_lanes(q, q)
    out[:q] = jnp.where(left, x[:q, :h], pltpu.roll(x[h : h + q, h:], q, 1))
    out[q:h] = x[q:h, :h]
    out[h : 2 * h] = x[h:, :h]
    out[2 * h : 2 * h + q] = x[h + q :, h:]
    out[2 * h + q :] = jnp.where(left_lanes(h, q), pltpu.roll(tail[:h], q, 1), tail[h:])


def unpack(m):
    h = 2 * m.shape[0] // 7
    q = h // 2
    left = left_lanes(q, q)
    first, low, last, tail = m[:h], m[h : 2 * h], m[2 * h : 2 * h + q], m[2 * h + q :]
    upper = jnp.concatenate([jnp.where(left, first[:q], first.T[:q]), first[q:]], axis=0)
    mirrored = jnp.concatenate([last, last], axis=0).T[:q]
    corner = jnp.concatenate([jnp.where(left, pltpu.roll(first[:q], q, 1), mirrored), last], axis=0)
    top = jnp.concatenate([upper, low.T], axis=1)
    bottom = jnp.concatenate([low, corner], axis=1)
    return jnp.concatenate([top, bottom], axis=0), jnp.concatenate([pltpu.roll(tail, q, 1), tail], axis=0)


def invert(d, guess, b, doublings, x_ref, finish):
    identity = unit(d.shape[0])
    d_parts = split(d, 3)
    b_parts = split(b, 3)
    guess_low = guess.astype(BF16)
    error = identity - one(d_parts[0], guess_low)
    power = error.astype(BF16)
    series = identity + error
    for _ in range(doublings):
        power = one(power, power).astype(BF16)
        series = series + one(series.astype(BF16), power)
    x = one(guess_low, series.astype(BF16))
    x_parts = split(x, 2)
    residual = identity - product(d_parts[:2], x_parts)
    x = x + one(x_parts[0], residual.astype(BF16))
    x_parts = split(x, 3)
    residual = identity - product(d_parts, x_parts)
    rest = residual.astype(BF16)
    y = product(x_parts, b_parts) + one(x_parts[0], one(rest, b_parts[0]).astype(BF16))
    finish(x + one(x_parts[0], rest), y)
    size = jnp.sum(residual * residual)

    @pl.when(jnp.logical_not(size < RESIDUAL_MAX * RESIDUAL_MAX))
    def _():
        x_ref[...] = jnp.where(size < 0.25, x, guess)

        def keep_on(state):
            step, worst = state
            return jnp.logical_and(step < SLOW_STEPS, worst > 1.0e-6)

        def improve(state):
            step, _ = state
            x = x_ref[...]
            rest = identity - product(d_parts, split(x, 3))
            x = x + product(split(x, 3), split(rest, 3))
            x_ref[...] = 0.5 * (x + x.T)
            return step + 1, jnp.sum(rest * rest)

        lax.while_loop(keep_on, improve, (0, jnp.float32(1.0)))
        finish(x_ref[...], product(split(x_ref[...], 3), b_parts))


def keep(x_ref, m_ref):
    def finish(x, y):
        x_ref[...] = x
        pack(x, y, m_ref)

    return finish


def first_guess(d):
    identity = unit(d.shape[0])
    diagonal = jnp.sum(d * identity, axis=1, keepdims=True)
    reach = jnp.max(jnp.sum(jnp.abs(d), axis=1, keepdims=True) / diagonal)
    return identity * (jnp.minimum(1.0, 1.9 / reach) / diagonal)


def start_kernel(doublings, d_ref, b_ref, m_ref, x_ref, b_out):
    d = d_ref[...]
    sides = b_ref[...]
    b = jnp.concatenate([jnp.zeros_like(sides), sides], axis=0).T
    b_out[...] = b
    invert(d, first_guess(d), b, doublings, x_ref, keep(x_ref, m_ref))


def reduce_rows(d_ref, b_ref, t_ref):
    half = t_ref.shape[0] // 2
    term, tail = unpack(t_ref[:half] + t_ref[half:])
    b = b_ref[...] - tail
    b = jnp.where(left_lanes(b.shape[0], b.shape[1] // 2), 0.0, b)
    return d_ref[...] - term, b


def level_kernel(doublings, stretch, d_ref, b_ref, t_ref, guess_ref, m_ref, x_ref, d_out, b_out):
    d, b = reduce_rows(d_ref, b_ref, t_ref)
    d_out[...] = d
    b_out[...] = b
    invert(d, stretch * guess_ref[...], b, doublings, x_ref, keep(x_ref, m_ref))


def end_kernel(doublings, stretch, info, d_ref, b_ref, t_ref, guess_ref, out_ref, x_ref):
    d, b = reduce_rows(d_ref, b_ref, t_ref)
    w = out_ref.shape[1]

    def finish(_, y):
        y = y.T
        out_ref[0] = jnp.where(info[1] == 0, y[2 * w : 3 * w], y[3 * w :])

    invert(d, stretch * guess_ref[...], b, doublings, x_ref, finish)


def transfer(c, m, t_ref):
    x, tail = unpack(m)
    c_parts = split(c, 3)
    z = product(c_parts, split(x, 3))
    pack(product(split(z, 3), c_parts, one_nt), product(c_parts, split(tail, 3)), t_ref)
    return z


def received(info, m_ref):
    return m_ref[...] if len(m_ref.shape) == 2 else jnp.where(info[1] == 0, m_ref[1], m_ref[0])


def following(z, far):
    return -product(split(z, 3), split(far, 3))


def first_coupling_kernel(info, m_ref, low_ref, near_ref, far_ref, t_ref, c_out):
    below = info[1] == 0
    c = jnp.where(below, low_ref[...], near_ref[...].T)
    c = jnp.where(jnp.logical_and(below, info[0] == 0), 0.0, c)
    far = far_ref[...]
    far = jnp.where(below, far, far.T)
    far = jnp.where(jnp.logical_and(below, info[0] == 1), 0.0, far)
    c_out[...] = following(transfer(c, received(info, m_ref), t_ref), far)


def coupling_kernel(info, m_ref, c_ref, t_ref, z_out):
    z_out[...] = transfer(c_ref[...], received(info, m_ref), t_ref)


def following_kernel(z_ref, far_ref, c_out):
    c_out[...] = following(z_ref[...], far_ref[...])


def last_coupling_kernel(m_ref, c_ref, t_ref):
    transfer(c_ref[...], m_ref[...], t_ref)


def call(kernel, name, operands, outs, scratch=(), scalars=False):
    specs = [pl.BlockSpec(memory_space=pltpu.VMEM)] * (len(operands) - int(scalars))
    if scalars:
        specs = [pl.BlockSpec(memory_space=pltpu.SMEM)] + specs
    shapes = [jax.ShapeDtypeStruct(shape, F32) for shape in outs]
    return pl.pallas_call(
        kernel,
        name=name,
        in_specs=specs,
        out_specs=[pl.BlockSpec(memory_space=pltpu.VMEM)] * len(outs),
        out_shape=shapes,
        scratch_shapes=[pltpu.VMEM(shape, F32) for shape in scratch],
        compiler_params=pltpu.CompilerParams(vmem_limit_bytes=40 * 2**20),
    )(*operands)


def pairs(line, stride):
    return [[2 * p, 2 * ((p - stride) % line) + 1] for p in range(line)]


def swapped(line, stride):
    both = [(2 * p, 2 * (p - stride) + 1) for p in range(stride, line)]
    return both + [(b, a) for a, b in both]


def outward(line, stride, core0, core1):
    route = []
    for p in range(line):
        if core0 and p + core0 * stride < line:
            route.append((2 * p, 2 * (p + core0 * stride)))
        if p - core1 * stride >= 0:
            route.append((2 * p + 1, 2 * (p - core1 * stride) + 1))
    return route


def on_device(diag_blocks, lower_blocks, right_sides):
    d, low, b = diag_blocks[0], lower_blocks[0], right_sides[0]
    n, w = b.shape
    line = lax.axis_size("line")
    info = jnp.stack([lax.axis_index("line"), lax.axis_index("rhs")]).astype(jnp.int32)
    near = lax.ppermute(low, BOTH, outward(line, 1, 0, 1))
    far = lax.ppermute(low, BOTH, outward(line, 1, 1, 2))
    sides = lax.all_gather(b.T, "rhs", tiled=True)
    square, tall, packed = (n, n), (n, 4 * w), (7 * n // 4, n // 2)
    level, stride = 0, 1
    message, x, b = call(
        functools.partial(start_kernel, DOUBLINGS[0]), "start", (d, sides), (packed, square, tall)
    )
    while stride < line:
        if level in GATHERED:
            near_m = lax.all_gather(message, BOTH, axis_index_groups=pairs(line, stride))
        else:
            near_m = lax.ppermute(message, BOTH, swapped(line, stride))
        if level > 1:
            (c,) = call(following_kernel, f"follow{level}", (z, far), (square,))
        if level in HELD:
            near_m, c = lax.optimization_barrier((near_m, c))
        if level == 0:
            term, c = call(
                first_coupling_kernel, "couple0", (info, near_m, low, near, far), (packed, square), scalars=True
            )
        elif 2 * stride < line:
            term, z = call(coupling_kernel, f"couple{level}", (info, near_m, c), (packed, square), scalars=True)
            far = lax.ppermute(c, BOTH, outward(line, stride, 1, 1))
        else:
            (term,) = call(last_coupling_kernel, f"couple{level}", (near_m, c), (packed,))
        terms = lax.all_gather(term, "rhs", tiled=True)
        level, stride = level + 1, 2 * stride
        place = min(level, len(DOUBLINGS) - 1)
        doublings, stretch = DOUBLINGS[place], STRETCH[place]
        if stride < line:
            message, x, d, b = call(
                functools.partial(level_kernel, doublings, stretch),
                f"invert{level}",
                (d, b, terms, x),
                (packed, square, square, tall),
            )
        else:
            (answer,) = call(
                functools.partial(end_kernel, doublings, stretch),
                "end",
                (info, d, b, terms, x),
                ((1, w, n),),
                scratch=(square,),
                scalars=True,
            )
    return jnp.swapaxes(answer, 1, 2)


def solution(mesh):
    placed = (P("line", None, None), P("line", None, None), P("line", None, "rhs"))
    return jax.shard_map(
        on_device, mesh=mesh, in_specs=placed, out_specs=P("line", None, "rhs"), check_vma=False
    )
```
